1024 devices in a mesh: rep: 64 (over z, core), tp: 16 (over y, x).
Axes of the slice: x: 4, y: 4, z: 32, core: 2. Of those that a mesh axis runs over, the one named last changes fastest.
Arguments:
- tokens: bfloat16 [3072, 3072], P('rep', 'tp'), may hold values from -6 to 6
- routes: int32 [3072, 4], P('rep'), may hold values from 0 to 31, all different within a row; in each aligned block of 48 rows (0 to 47, 48 to 95, ...) at most 12 rows name the same one
- gates: float32 [3072, 4], P('rep'), may hold values from 0.1 to 1
- w_gate: bfloat16 [64, 3072, 3072], P('rep', None, 'tp'), may hold values from -0.109375 to 0.109375
- w_up: bfloat16 [64, 3072, 3072], P('rep', None, 'tp'), may hold values from -0.109375 to 0.109375
- w_down: bfloat16 [64, 3072, 3072], P('rep', 'tp'), may hold values from -0.078125 to 0.078125
Outputs:
- mixed: bfloat16 [3072, 3072], P('rep', 'tp')
The draws below stay inside these ranges and needn't reach their ends.
Inputs may be any that keep to these rules, and one draw needn't show every extreme that they name: `routes`: A token's 4 slots are different. Among the 48 tokens of one index of rep, no slot is named by more than 12 choices, a bound that some block reaches.
All inputs are finite; a program needn't handle non-finite values.
Results may differ from the reference program's by a relative error of at most 0.019.
Values may be sent and summed in bfloat16 or wider, within the bound.
No kernel may reach another device: no remote copies, remote signals or barrier semaphores. Data moves between devices by JAX's collectives and lax.ppermute only.
A program may use at most 32 MiB of HBM per device.

```python
import math
import jax
import jax.numpy as jnp
import numpy as np
from jax import lax

D = 3072
FF_DEV = 192
FF = 6144
TOP = 4
SLOTS = 32
TOK_DEV = 48
TOKENS = 3072
CAP = 12
N_REP = 64
N_TP = 16


def steps_of(stream_key, dims, split, low, largest):
    factor_of, own = 1.0, jax.random.fold_in(stream_key, 6)
    for dim, blocks in split:
        draws = jnp.exp(jax.random.uniform(jax.random.fold_in(own, dim), (blocks,), jnp.float32, low / len(split), largest / len(split)))
        factor_of = factor_of * jnp.repeat(draws, dims[dim] // blocks).reshape([-1 if axis == dim else 1 for axis in range(len(dims))])
    return factor_of


def deal_out(key, own, number, rows, count, top, reach, skew):
    sequence = jax.random.permutation(key, count)
    crowded, usual = portions_of(count, rows * top, reach, skew, True), portions_of(count, rows * top, reach, skew, False)
    places = jnp.arange(count)

    def named(tallies, rotation):
        used = int((tallies > 0).sum())
        fixed = max(1, used // 4)
        moved = fixed + (places - fixed + rotation * (used - fixed)) % max(1, count - fixed)
        return jnp.zeros((count,), jnp.int32).at[sequence[jnp.where(places < fixed, places, moved)]].set(jnp.asarray(tallies, jnp.int32))

    tallies = jnp.where(number % 4 == 0, named(crowded, number // 4), named(usual, number - number // 4 - 1))
    mixed = jax.random.permutation(jax.random.fold_in(own, 3), count)
    source_of, receiver = mixed[0:count // 2 * 2:2], mixed[1:count // 2 * 2:2]
    margin = jnp.minimum(tallies[source_of] - 1, reach - tallies[receiver]) // 2
    margin = jnp.where((source_of == sequence[0]) | (receiver == sequence[0]) | (tallies[receiver] == 0), 0, jnp.maximum(margin, 0))
    moved = jax.random.randint(jax.random.fold_in(own, 4), (count // 2,), 0, 1 << 20) % (margin + 1)
    tallies = tallies.at[source_of].add(-moved).at[receiver].add(moved)
    members = jnp.searchsorted(jnp.cumsum(tallies), jnp.arange(rows * top), side="right").astype(jnp.int32)
    grid = members.reshape(top, rows).T
    grid = grid[jax.random.permutation(jax.random.fold_in(own, 1), rows)]
    rotation = jax.random.randint(jax.random.fold_in(own, 2), (rows, 1), 0, top)
    return jnp.take_along_axis(grid, (jnp.arange(top)[None, :] + rotation) % top, axis=1)


def portions_of(amount, total, bound, slope, full):
    portions = [(1 << 20) // math.isqrt(grade ** slope) + 1 for grade in range(1, amount + 1)]
    largest = bound if full else min(bound, max(-(-total // amount), total * portions[0] // sum(portions)))
    least = 1 if total - largest >= amount - 1 else 0
    given, surplus = [largest] + [least] * (amount - 1), total - largest - least * (amount - 1)
    while surplus > 0:
        free = [i for i in range(1, amount) if given[i] < largest] or [i for i in range(1, amount) if given[i] < bound]
        pool, left = sum([portions[i] for i in free]), surplus
        for i in free:
            more = min(bound - given[i], max(1, left * portions[i] // pool), surplus)
            given[i] = given[i] + more
            surplus = surplus - more
    return np.array(given)


def normal_values(stream_key, shape, width, most, split=(), kind=jnp.bfloat16):
    loudness = steps_of(stream_key, shape, split, -0.22, 0.18) if split else 1.0
    result = jax.random.normal(stream_key, shape, jnp.float32) * width * loudness
    return jnp.minimum(jnp.maximum(result, -most), most).astype(kind)


def setup_inputs(seed: int = 0) -> dict:
    seeds = jax.random.split(jax.random.key(seed), 7)
    tokens = normal_values(seeds[0], (TOKENS, D), 1.0, 6.0, ((0, 64), (1, 16)))
    routes_keys = jax.random.split(jax.random.fold_in(seeds[1], 1), TOKENS // TOK_DEV)
    routes_turns = jax.random.permutation(jax.random.fold_in(seeds[1], 3), TOKENS // TOK_DEV)
    routes = jax.vmap(lambda own, number: deal_out(jax.random.fold_in(seeds[1], 2), own, number, TOK_DEV, SLOTS, TOP, CAP, 2))(routes_keys, routes_turns).reshape((TOKENS, TOP))
    gates = jnp.clip(jnp.exp(math.log(1.0) - 2.3025851 * jax.random.uniform(seeds[2], (TOKENS, TOP), jnp.float32) ** steps_of(seeds[2], (TOKENS, TOP), ((0, 64),), -0.2, 0.2)), 0.1, 1.0)
    w_gate = normal_values(seeds[3], (N_REP, D, FF // 2), D ** -0.5, 0.109375, ((0, 64), (2, 16)))
    w_up = normal_values(seeds[4], (N_REP, D, FF // 2), D ** -0.5, 0.109375, ((0, 64), (2, 16)))
    w_down = normal_values(seeds[5], (N_REP, FF // 2, D), FF ** -0.5, 0.078125, ((0, 64), (1, 16)))
    return {"tokens": tokens, "routes": routes, "gates": gates, "w_gate": w_gate, "w_up": w_up, "w_down": w_down}


def reference(tokens, routes, gates, w_gate, w_up, w_down):
    flat_slot = routes.reshape(-1).astype(jnp.int32)
    flat_gate = gates.reshape(-1)
    entries = TOKENS * TOP
    slot_rows = N_REP * CAP
    order_all = jnp.arange(entries, dtype=jnp.int32)

    def one_half(row_data, index):
        gate_acc = jnp.dot(row_data, w_gate[index], preferred_element_type=jnp.float32)
        up_acc = jnp.dot(row_data, w_up[index], preferred_element_type=jnp.float32)
        hidden = (jax.nn.silu(gate_acc) * up_acc).astype(jnp.bfloat16)
        hidden_f = hidden.reshape(slot_rows, N_TP, FF_DEV).transpose(1, 0, 2).astype(jnp.float32)
        down_f = w_down[index].reshape(N_TP, FF_DEV, D).astype(jnp.float32)
        partials = jnp.einsum("pmf,pfd->pmd", hidden_f, down_f).astype(jnp.bfloat16)
        partials = lax.optimization_barrier(partials).astype(jnp.float32)
        return jnp.sum(partials, axis=0).astype(jnp.bfloat16).astype(jnp.float32)

    def one_slot(totals, slot_id):
        sort_keys = jnp.where(flat_slot == slot_id, order_all, entries + order_all)
        picked = jnp.argsort(sort_keys)[:slot_rows].astype(jnp.int32)
        is_live = (flat_slot[picked] == slot_id).astype(jnp.float32)
        owners = (picked // TOP).astype(jnp.int32)
        row_data = tokens[owners]
        expert_out = one_half(row_data, 2 * slot_id) + one_half(row_data, 2 * slot_id + 1)
        weight = flat_gate[picked] * is_live
        contrib = weight[:, None] * expert_out
        return totals.at[owners].add(contrib), None

    start = jnp.zeros((TOKENS, D), jnp.float32)
    totals, unused = lax.scan(one_slot, start, jnp.arange(SLOTS, dtype=jnp.int32))
    return totals.astype(jnp.bfloat16)
```

```python
import functools

import jax
import jax.numpy as jnp
from jax import lax
from jax.experimental import pallas as pl
from jax.experimental.pallas import tpu as pltpu
from jax.sharding import Mesh
from jax.sharding import PartitionSpec as P

LANES = 128
HALF = LANES // 2
SHARE = LANES + HALF
F32 = jnp.float32
BF16 = jnp.bfloat16


def iota(shape, dim):
    return lax.broadcasted_iota(jnp.int32, shape, dim)


def lines_of(slot, place, cap):
    half, lines = cap // 2, 3 * cap // 2
    start = slot * lines
    head = start + place
    low = jnp.where(place < half, start + cap + place, -1)
    high = jnp.where(place < half, -1, start + cap + place - half)
    return head, low, high


def dispatch_kernel(slots, cap, tokens_ref, routes_ref, out_ref):
    odd = lax.rem(lax.axis_index("x"), 2) == 1
    count = tokens_ref.shape[0]
    top = routes_ref.shape[0]
    total = slots * cap * 3 // 2
    tok = tokens_ref[...].astype(F32)
    head = jnp.where(odd, tok[:, HALF:], tok[:, :LANES])
    tail = jnp.where(odd, tok[:, :HALF], tok[:, LANES:])
    both = jnp.concatenate([tail, tail], axis=1)
    left = iota((count, LANES), 1) < HALF
    chosen = [routes_ref[k : k + 1, :] for k in range(top)]
    slot_ids = iota((slots, count), 0)
    onehots = [chosen[k] == slot_ids for k in range(top)]
    named = functools.reduce(jnp.logical_or, onehots).astype(F32).astype(BF16)
    earlier = (iota((count, count), 0) < iota((count, count), 1)).astype(F32).astype(BF16)
    before = jnp.dot(named, earlier, preferred_element_type=F32)
    line_ids = iota((total, count), 0)
    masks = [None, None, None]
    for k in range(top):
        place = jnp.sum(jnp.where(onehots[k], before, 0.0), axis=0, keepdims=True).astype(jnp.int32)
        for n, line in enumerate(lines_of(chosen[k], place, cap)):
            hit = line_ids == line
            masks[n] = hit if masks[n] is None else jnp.logical_or(masks[n], hit)
    parts = (head, jnp.where(left, both, 0.0), jnp.where(left, 0.0, both))
    out = jnp.zeros((total, LANES), F32)
    for mask, part in zip(masks, parts):
        out = out + jnp.dot(
            mask.astype(F32).astype(BF16), part.astype(BF16), preferred_element_type=F32
        )
    out_ref[...] = out.astype(BF16)


def spread_kernel(cap, in_ref, out_ref):
    total = in_ref.shape[0]
    half, group = cap // 2, in_ref.shape[0] // 3
    place = iota((total, 1), 0)
    kind, rest = place // group, place % group
    source = rest // half * (3 * half) + rest % half + kind * half
    order = (source == iota((total, total), 1)).astype(F32).astype(BF16)
    lines = jnp.dot(order, in_ref[...], preferred_element_type=F32).astype(BF16)
    for n in range(out_ref.shape[0]):
        out_ref[n] = lines


def ffn_kernel(x_ref, gate_ref, up_ref, down_ref, out_ref, rows_ref):
    rows = rows_ref.shape[0]
    mid = rows // 2
    left = iota((mid, LANES), 1) < HALF
    pairs = x_ref.shape[0] // 2
    wide = 3 * LANES
    for n in range(pairs):
        start = n * wide
        rows_ref[:, start : start + LANES] = x_ref[2 * n, :rows, :]
        rows_ref[:, start + 2 * LANES : start + wide] = x_ref[2 * n + 1, :rows, :]
        a = x_ref[2 * n, rows:, :].astype(F32)
        b = x_ref[2 * n + 1, rows:, :].astype(F32)
        upper = jnp.where(left, a, pltpu.roll(b, HALF, 1))
        lower = jnp.where(left, pltpu.roll(a, HALF, 1), b)
        rows_ref[:mid, start + LANES : start + 2 * LANES] = upper.astype(BF16)
        rows_ref[mid:, start + LANES : start + 2 * LANES] = lower.astype(BF16)
    hidden = []
    last = (((1,), (1,)), ((), ()))
    for h in range(2):
        gate = lax.dot_general(rows_ref[...], gate_ref[h], last, preferred_element_type=F32)
        up = lax.dot_general(rows_ref[...], up_ref[h], last, preferred_element_type=F32)
        hidden.append((gate / (1.0 + jnp.exp(-gate)) * up).astype(BF16))
    for n in range(pairs):
        start = n * wide
        out = jnp.dot(hidden[0], down_ref[0, :, start : start + wide], preferred_element_type=F32)
        out = out + jnp.dot(
            hidden[1], down_ref[1, :, start : start + wide], preferred_element_type=F32
        )
        out_ref[2 * n, :rows, :] = out[:, :LANES].astype(BF16)
        out_ref[2 * n + 1, :rows, :] = out[:, 2 * LANES :].astype(BF16)
        upper, lower = out[:mid, LANES : 2 * LANES], out[mid:, LANES : 2 * LANES]
        out_ref[2 * n, rows:, :] = jnp.where(left, upper, pltpu.roll(lower, HALF, 1)).astype(BF16)
        out_ref[2 * n + 1, rows:, :] = jnp.where(left, pltpu.roll(upper, HALF, 1), lower).astype(
            BF16
        )


def sum_kernel(cap, in_ref, out_ref):
    total = in_ref.shape[1]
    half, group = cap // 2, total // 3
    acc = in_ref[0].astype(F32)
    for n in range(1, in_ref.shape[0]):
        acc = acc + in_ref[n].astype(F32)
    place = iota((total, 1), 0)
    block, line = place // (3 * half), place % (3 * half)
    source = line // half * group + block * half + line % half
    order = (source == iota((total, total), 1)).astype(F32).astype(BF16)
    out_ref[...] = jnp.dot(order, acc.astype(BF16), preferred_element_type=F32).astype(BF16)


def combine_kernel(slots, cap, in_ref, routes_ref, gates_ref, out_ref):
    odd = lax.rem(lax.axis_index("x"), 2) == 1
    count, top = routes_ref.shape
    total = in_ref.shape[0]
    slot_ids = iota((count, slots), 1)
    chosen = [routes_ref[:, k : k + 1] for k in range(top)]
    onehots = [chosen[k] == slot_ids for k in range(top)]
    named = functools.reduce(jnp.logical_or, onehots).astype(F32).astype(BF16)
    earlier = (iota((count, count), 0) > iota((count, count), 1)).astype(F32).astype(BF16)
    before = jnp.dot(earlier, named, preferred_element_type=F32)
    line_ids = iota((count, total), 1)
    weights = [jnp.zeros((count, total), F32) for _ in range(3)]
    for k in range(top):
        place = jnp.sum(jnp.where(onehots[k], before, 0.0), axis=1, keepdims=True).astype(jnp.int32)
        for n, line in enumerate(lines_of(chosen[k], place, cap)):
            weights[n] = jnp.where(line_ids == line, gates_ref[:, k : k + 1], weights[n])
    lines = in_ref[...]
    sums = []
    for weight in weights:
        coarse = weight.astype(BF16)
        fine = (weight - coarse.astype(F32)).astype(BF16)
        sums.append(
            jnp.dot(coarse, lines, preferred_element_type=F32)
            + jnp.dot(fine, lines, preferred_element_type=F32)
        )
    head, tail = sums[0], sums[1][:, :HALF] + sums[2][:, HALF:]
    out = jnp.where(
        odd, jnp.concatenate([tail, head], axis=1), jnp.concatenate([head, tail], axis=1)
    )
    out_ref[...] = out.astype(BF16)


def call(kernel, shape, *args, scratch=(), limit=16, flops=0):
    vmem = pl.BlockSpec(memory_space=pltpu.VMEM)
    size = sum(a.size * a.dtype.itemsize for a in args)
    return pl.pallas_call(
        kernel,
        out_shape=jax.ShapeDtypeStruct(shape, BF16),
        in_specs=[vmem] * len(args),
        out_specs=vmem,
        scratch_shapes=list(scratch),
        compiler_params=pltpu.CompilerParams(vmem_limit_bytes=limit * 1024 * 1024),
        cost_estimate=pl.CostEstimate(flops=flops, bytes_accessed=size, transcendentals=0),
    )(*args)


def exchange_z(lines, slots):
    blocks = lines.reshape(slots, -1, 2, LANES)
    return lax.all_to_all(blocks, "z", split_axis=0, concat_axis=0, tiled=True).reshape(lines.shape)


def per_device(tokens, routes, gates, w_gate, w_up, w_down):
    slots = lax.axis_size("z")
    shares = lax.axis_size("y") * lax.axis_size("x")
    count, top = routes.shape
    cap = min(count, 2 * count * top // slots)
    total = slots * cap * 3 // 2
    rows = slots * cap
    gate_all = lax.all_gather(w_gate.swapaxes(1, 2), "core", axis=0, tiled=True)
    up_all = lax.all_gather(w_up.swapaxes(1, 2), "core", axis=0, tiled=True)
    down_all = lax.all_gather(w_down, "core", axis=0, tiled=True)
    outgoing = call(
        functools.partial(dispatch_kernel, slots, cap), (total, LANES), tokens, routes.T
    )
    incoming = exchange_z(outgoing, slots)
    copies = call(functools.partial(spread_kernel, cap), (shares, total, LANES), incoming)
    features = lax.all_to_all(copies, ("y", "x"), split_axis=0, concat_axis=0, tiled=True)
    partials = call(
        ffn_kernel,
        (shares, total, LANES),
        features,
        gate_all,
        up_all,
        down_all,
        scratch=[pltpu.VMEM((rows, shares * SHARE), BF16)],
        limit=40,
        flops=2 * rows * shares * SHARE * 6 * SHARE,
    )
    landed = lax.all_to_all(partials, ("y", "x"), split_axis=0, concat_axis=0, tiled=True)
    summed = call(functools.partial(sum_kernel, cap), (total, LANES), landed)
    returned = exchange_z(summed, slots)
    return call(
        functools.partial(combine_kernel, slots, cap), (count, SHARE), returned, routes, gates
    )


def split_mesh(mesh):
    reps, shares = mesh.devices.shape
    side = int(round(shares**0.5))
    return Mesh(mesh.devices.reshape(reps // 2, 2, side, -1), ("z", "core", "y", "x"))


def solution(mesh):
    rep, tp = ("z", "core"), ("y", "x")
    in_specs = (
        P(rep, tp),
        P(rep, None),
        P(rep, None),
        P(rep, None, tp),
        P(rep, None, tp),
        P(rep, tp, None),
    )
    return jax.shard_map(
        per_device,
        mesh=split_mesh(mesh),
        in_specs=in_specs,
        out_specs=P(rep, tp),
        check_vma=False,
    )
```

```python
import functools

import jax
import jax.numpy as jnp
from jax import lax
from jax.experimental import pallas as pl
from jax.experimental.pallas import tpu as pltpu
from jax.sharding import Mesh
from jax.sharding import PartitionSpec as P

LANES = 128
HALF = LANES // 2
SHARE = LANES + HALF
F32 = jnp.float32
BF16 = jnp.bfloat16


def iota(shape, dim):
    return lax.broadcasted_iota(jnp.int32, shape, dim)


def lines_of(slot, place, cap):
    half, lines = cap // 2, 3 * cap // 2
    start = slot * lines
    head = start + place
    low = jnp.where(place < half, start + cap + place, -1)
    high = jnp.where(place < half, -1, start + cap + place - half)
    return head, low, high


def dispatch_kernel(slots, cap, tokens_ref, routes_ref, gates_ref, out_ref, weights_ref):
    odd = lax.rem(lax.axis_index("x"), 2) == 1
    count = tokens_ref.shape[0]
    top = routes_ref.shape[0]
    total = slots * cap * 3 // 2
    tok = tokens_ref[...].astype(F32)
    head = jnp.where(odd, tok[:, HALF:], tok[:, :LANES])
    tail = jnp.where(odd, tok[:, :HALF], tok[:, LANES:])
    both = jnp.concatenate([tail, tail], axis=1)
    left = iota((count, LANES), 1) < HALF
    chosen = [routes_ref[k : k + 1, :] for k in range(top)]
    slot_ids = iota((slots, count), 0)
    onehots = [chosen[k] == slot_ids for k in range(top)]
    named = functools.reduce(jnp.logical_or, onehots).astype(F32).astype(BF16)
    earlier = (iota((count, count), 0) < iota((count, count), 1)).astype(F32).astype(BF16)
    before = jnp.dot(named, earlier, preferred_element_type=F32)
    line_ids = iota((total, count), 0)
    lane_ids = iota((count, total), 1)
    diagonal = iota((count, count), 0) == iota((count, count), 1)

    def column(row):
        return jnp.sum(jnp.where(diagonal, row, 0.0), axis=1, keepdims=True)

    masks = [None, None, None]
    weights = [jnp.zeros((count, total), F32) for _ in range(3)]
    for k in range(top):
        place = jnp.sum(jnp.where(onehots[k], before, 0.0), axis=0, keepdims=True)
        slot_column = column(chosen[k].astype(F32)).astype(jnp.int32)
        place_column = column(place).astype(jnp.int32)
        gate_column = column(gates_ref[k : k + 1, :])
        place = place.astype(jnp.int32)
        for n, line in enumerate(lines_of(chosen[k], place, cap)):
            hit = line_ids == line
            masks[n] = hit if masks[n] is None else jnp.logical_or(masks[n], hit)
        for n, line in enumerate(lines_of(slot_column, place_column, cap)):
            weights[n] = jnp.where(lane_ids == line, gate_column, weights[n])
    parts = (head, jnp.where(left, both, 0.0), jnp.where(left, 0.0, both))
    out = jnp.zeros((total, LANES), F32)
    for mask, part in zip(masks, parts):
        out = out + jnp.dot(
            mask.astype(F32).astype(BF16), part.astype(BF16), preferred_element_type=F32
        )
    out_ref[...] = out.astype(BF16)
    for n, weight in enumerate(weights):
        coarse = weight.astype(BF16)
        weights_ref[n * count : (n + 1) * count, :] = coarse
        weights_ref[(n + 3) * count : (n + 4) * count, :] = (weight - coarse.astype(F32)).astype(
            BF16
        )


def spread_kernel(cap, in_ref, out_ref):
    total = in_ref.shape[0]
    half, group = cap // 2, in_ref.shape[0] // 3
    place = iota((total, 1), 0)
    kind, rest = place // group, place % group
    source = rest // half * (3 * half) + rest % half + kind * half
    order = (source == iota((total, total), 1)).astype(F32).astype(BF16)
    lines = jnp.dot(order, in_ref[...], preferred_element_type=F32).astype(BF16)
    for n in range(out_ref.shape[0]):
        out_ref[n] = lines


def ffn_kernel(x_ref, gate_ref, up_ref, down_ref, other_ref, out_ref, rows_ref):
    rows = rows_ref.shape[0]
    mid = rows // 2
    left = iota((mid, LANES), 1) < HALF
    pairs = x_ref.shape[0] // 2
    wide = 3 * LANES
    for n in range(pairs):
        start = n * wide
        rows_ref[:, start : start + LANES] = x_ref[2 * n, :rows, :]
        rows_ref[:, start + 2 * LANES : start + wide] = x_ref[2 * n + 1, :rows, :]
        a = x_ref[2 * n, rows:, :].astype(F32)
        b = x_ref[2 * n + 1, rows:, :].astype(F32)
        upper = jnp.where(left, a, pltpu.roll(b, HALF, 1))
        lower = jnp.where(left, pltpu.roll(a, HALF, 1), b)
        rows_ref[:mid, start + LANES : start + 2 * LANES] = upper.astype(BF16)
        rows_ref[mid:, start + LANES : start + 2 * LANES] = lower.astype(BF16)
    hidden = []
    last = (((1,), (1,)), ((), ()))
    for gates, ups in ((gate_ref[0], up_ref[0]), (other_ref[0], other_ref[1])):
        gate = lax.dot_general(rows_ref[...], gates, last, preferred_element_type=F32)
        up = lax.dot_general(rows_ref[...], ups, last, preferred_element_type=F32)
        hidden.append((gate / (1.0 + jnp.exp(-gate)) * up).astype(BF16))
    for n in range(pairs):
        start = n * wide
        out = jnp.dot(hidden[0], down_ref[0, :, start : start + wide], preferred_element_type=F32)
        out = out + jnp.dot(
            hidden[1], other_ref[2, :, start : start + wide], preferred_element_type=F32
        )
        out_ref[2 * n, :rows, :] = out[:, :LANES].astype(BF16)
        out_ref[2 * n + 1, :rows, :] = out[:, 2 * LANES :].astype(BF16)
        upper, lower = out[:mid, LANES : 2 * LANES], out[mid:, LANES : 2 * LANES]
        out_ref[2 * n, rows:, :] = jnp.where(left, upper, pltpu.roll(lower, HALF, 1)).astype(BF16)
        out_ref[2 * n + 1, rows:, :] = jnp.where(left, pltpu.roll(upper, HALF, 1), lower).astype(
            BF16
        )


def sum_kernel(cap, in_ref, out_ref):
    total = in_ref.shape[1]
    half, group = cap // 2, total // 3
    acc = in_ref[0].astype(F32)
    for n in range(1, in_ref.shape[0]):
        acc = acc + in_ref[n].astype(F32)
    place = iota((total, 1), 0)
    block, line = place // (3 * half), place % (3 * half)
    source = line // half * group + block * half + line % half
    order = (source == iota((total, total), 1)).astype(F32).astype(BF16)
    out_ref[...] = jnp.dot(order, acc.astype(BF16), preferred_element_type=F32).astype(BF16)


def combine_kernel(in_ref, weights_ref, out_ref):
    odd = lax.rem(lax.axis_index("x"), 2) == 1
    count = out_ref.shape[0]
    sums = jnp.dot(weights_ref[...], in_ref[...], preferred_element_type=F32)
    sums = sums[: 3 * count] + sums[3 * count :]
    head = sums[:count]
    tail = sums[count : 2 * count, :HALF] + sums[2 * count :, HALF:]
    out = jnp.where(
        odd, jnp.concatenate([tail, head], axis=1), jnp.concatenate([head, tail], axis=1)
    )
    out_ref[...] = out.astype(BF16)


def call(kernel, shapes, *args, scratch=(), limit=16, flops=0):
    vmem = pl.BlockSpec(memory_space=pltpu.VMEM)
    size = sum(a.size * a.dtype.itemsize for a in args)
    outs = pl.pallas_call(
        kernel,
        out_shape=[jax.ShapeDtypeStruct(shape, BF16) for shape in shapes],
        in_specs=[vmem] * len(args),
        out_specs=[vmem] * len(shapes),
        scratch_shapes=list(scratch),
        compiler_params=pltpu.CompilerParams(vmem_limit_bytes=limit * 1024 * 1024),
        cost_estimate=pl.CostEstimate(flops=flops, bytes_accessed=size, transcendentals=0),
    )(*args)
    return outs if len(shapes) > 1 else outs[0]


def exchange_z(lines, slots):
    blocks = lines.reshape(slots, -1, 2, LANES)
    return lax.all_to_all(blocks, "z", split_axis=0, concat_axis=0, tiled=True).reshape(lines.shape)


def per_device(tokens, routes, gates, w_gate, w_up, w_down):
    slots = lax.axis_size("z")
    shares = lax.axis_size("y") * lax.axis_size("x")
    count, top = routes.shape
    cap = min(count, 2 * count * top // slots)
    total = slots * cap * 3 // 2
    rows = slots * cap
    own = [w_gate.swapaxes(1, 2), w_up.swapaxes(1, 2), w_down]
    other = lax.ppermute(jnp.concatenate(own, axis=0), "core", [(0, 1), (1, 0)])
    outgoing, weights = call(
        functools.partial(dispatch_kernel, slots, cap),
        [(total, LANES), (6 * count, total)],
        tokens,
        routes.T,
        gates.T,
    )
    incoming = exchange_z(outgoing, slots)
    copies = call(functools.partial(spread_kernel, cap), [(shares, total, LANES)], incoming)
    features = lax.all_to_all(copies, ("y", "x"), split_axis=0, concat_axis=0, tiled=True)
    partials = call(
        ffn_kernel,
        [(shares, total, LANES)],
        features,
        *own,
        other,
        scratch=[pltpu.VMEM((rows, shares * SHARE), BF16)],
        limit=32,
        flops=2 * rows * shares * SHARE * 6 * SHARE,
    )
    landed = lax.all_to_all(partials, ("y", "x"), split_axis=0, concat_axis=0, tiled=True)
    summed = call(functools.partial(sum_kernel, cap), [(total, LANES)], landed)
    returned = exchange_z(summed, slots)
    return call(combine_kernel, [(count, SHARE)], returned, weights)


def split_mesh(mesh):
    reps, shares = mesh.devices.shape
    side = int(round(shares**0.5))
    return Mesh(mesh.devices.reshape(reps // 2, 2, side, -1), ("z", "core", "y", "x"))


def solution(mesh):
    rep, tp = ("z", "core"), ("y", "x")
    in_specs = (
        P(rep, tp),
        P(rep, None),
        P(rep, None),
        P(rep, None, tp),
        P(rep, None, tp),
        P(rep, tp, None),
    )
    return jax.shard_map(
        per_device,
        mesh=split_mesh(mesh),
        in_specs=in_specs,
        out_specs=P(rep, tp),
        check_vma=False,
    )
```

```python
import functools

import jax
import jax.numpy as jnp
from jax import lax
from jax.experimental import pallas as pl
from jax.experimental.pallas import tpu as pltpu
from jax.sharding import Mesh
from jax.sharding import PartitionSpec as P

LANES = 128
HALF = LANES // 2
SHARE = LANES + HALF
F32 = jnp.float32
BF16 = jnp.bfloat16


def iota(shape, dim):
    return lax.broadcasted_iota(jnp.int32, shape, dim)


def lines_of(slot, place, cap):
    half, lines = cap // 2, 3 * cap // 2
    start = slot * lines
    head = start + place
    low = jnp.where(place < half, start + cap + place, -1)
    high = jnp.where(place < half, -1, start + cap + place - half)
    return head, low, high


def dispatch_kernel(
    slots,
    cap,
    tokens_ref,
    routes_ref,
    gates_ref,
    w_gate_ref,
    w_up_ref,
    w_down_ref,
    out_ref,
    weights_ref,
    own_ref,
    sems,
):
    copies = [
        pltpu.make_async_copy(ref.at[0], own_ref.at[n], sems.at[n])
        for n, ref in enumerate((w_gate_ref, w_up_ref, w_down_ref))
    ]
    for copy in copies:
        copy.start()
    odd = lax.rem(lax.axis_index("x"), 2) == 1
    count = tokens_ref.shape[0]
    top = routes_ref.shape[0]
    total = slots * cap * 3 // 2
    tok = tokens_ref[...].astype(F32)
    head = jnp.where(odd, tok[:, HALF:], tok[:, :LANES])
    tail = jnp.where(odd, tok[:, :HALF], tok[:, LANES:])
    both = jnp.concatenate([tail, tail], axis=1)
    left = iota((count, LANES), 1) < HALF
    chosen = [routes_ref[k : k + 1, :] for k in range(top)]
    slot_ids = iota((slots, count), 0)
    onehots = [chosen[k] == slot_ids for k in range(top)]
    named = functools.reduce(jnp.logical_or, onehots).astype(F32).astype(BF16)
    earlier = (iota((count, count), 0) < iota((count, count), 1)).astype(F32).astype(BF16)
    before = jnp.dot(named, earlier, preferred_element_type=F32)
    line_ids = iota((total, count), 0)
    lane_ids = iota((count, total), 1)
    diagonal = iota((count, count), 0) == iota((count, count), 1)

    def column(row):
        return jnp.sum(jnp.where(diagonal, row, 0.0), axis=1, keepdims=True)

    masks = [None, None, None]
    weights = [jnp.zeros((count, total), F32) for _ in range(3)]
    for k in range(top):
        place = jnp.sum(jnp.where(onehots[k], before, 0.0), axis=0, keepdims=True)
        slot_column = column(chosen[k].astype(F32)).astype(jnp.int32)
        place_column = column(place).astype(jnp.int32)
        gate_column = column(gates_ref[k : k + 1, :])
        place = place.astype(jnp.int32)
        for n, line in enumerate(lines_of(chosen[k], place, cap)):
            hit = line_ids == line
            masks[n] = hit if masks[n] is None else jnp.logical_or(masks[n], hit)
        for n, line in enumerate(lines_of(slot_column, place_column, cap)):
            weights[n] = jnp.where(lane_ids == line, gate_column, weights[n])
    parts = (head, jnp.where(left, both, 0.0), jnp.where(left, 0.0, both))
    out = jnp.zeros((total, LANES), F32)
    for mask, part in zip(masks, parts):
        out = out + jnp.dot(
            mask.astype(F32).astype(BF16), part.astype(BF16), preferred_element_type=F32
        )
    out_ref[...] = out.astype(BF16)
    for n, weight in enumerate(weights):
        coarse = weight.astype(BF16)
        weights_ref[n * count : (n + 1) * count, :] = coarse
        weights_ref[(n + 3) * count : (n + 4) * count, :] = (weight - coarse.astype(F32)).astype(
            BF16
        )
    for copy in copies:
        copy.wait()


def spread_kernel(cap, in_ref, out_ref):
    total = in_ref.shape[1]
    half, group = cap // 2, total // 3
    place = iota((total, 1), 0)
    kind, rest = place // group, place % group
    source = rest // half * (3 * half) + rest % half + kind * half
    order = (source == iota((total, total), 1)).astype(F32).astype(BF16)
    for share in range(in_ref.shape[0]):
        lines = jnp.dot(order, in_ref[share], preferred_element_type=F32).astype(BF16)
        for n in range(out_ref.shape[0]):
            out_ref[n, share] = lines


def ffn_kernel(x_ref, own_ref, other_ref, out_ref, rows_ref):
    side = x_ref.shape[0]
    first = lax.axis_index("core") == 0

    def block(n):
        y, x = n // side, n % side
        return jnp.where(first, y, x), jnp.where(first, x, y)

    rows = rows_ref.shape[0]
    mid = rows // 2
    left = iota((mid, LANES), 1) < HALF
    pairs = out_ref.shape[0] // 2
    wide = 3 * LANES
    for n in range(pairs):
        start = n * wide
        even, odd = block(2 * n), block(2 * n + 1)
        rows_ref[:, start : start + LANES] = x_ref[even[0], even[1], :rows, :]
        rows_ref[:, start + 2 * LANES : start + wide] = x_ref[odd[0], odd[1], :rows, :]
        a = x_ref[even[0], even[1], rows:, :].astype(F32)
        b = x_ref[odd[0], odd[1], rows:, :].astype(F32)
        upper = jnp.where(left, a, pltpu.roll(b, HALF, 1))
        lower = jnp.where(left, pltpu.roll(a, HALF, 1), b)
        rows_ref[:mid, start + LANES : start + 2 * LANES] = upper.astype(BF16)
        rows_ref[mid:, start + LANES : start + 2 * LANES] = lower.astype(BF16)
    hidden = []
    last = (((1,), (1,)), ((), ()))
    for gates, ups in ((own_ref[0], own_ref[1]), (other_ref[0], other_ref[1])):
        gate = lax.dot_general(rows_ref[...], gates, last, preferred_element_type=F32)
        up = lax.dot_general(rows_ref[...], ups, last, preferred_element_type=F32)
        hidden.append((gate / (1.0 + jnp.exp(-gate)) * up).astype(BF16))
    for n in range(pairs):
        start = n * wide
        out = jnp.dot(hidden[0], own_ref[2, :, start : start + wide], preferred_element_type=F32)
        out = out + jnp.dot(
            hidden[1], other_ref[2, :, start : start + wide], preferred_element_type=F32
        )
        out_ref[2 * n, :rows, :] = out[:, :LANES].astype(BF16)
        out_ref[2 * n + 1, :rows, :] = out[:, 2 * LANES :].astype(BF16)
        upper, lower = out[:mid, LANES : 2 * LANES], out[mid:, LANES : 2 * LANES]
        out_ref[2 * n, rows:, :] = jnp.where(left, upper, pltpu.roll(lower, HALF, 1)).astype(BF16)
        out_ref[2 * n + 1, rows:, :] = jnp.where(left, pltpu.roll(upper, HALF, 1), lower).astype(
            BF16
        )


def sum_kernel(cap, in_ref, out_ref):
    total = in_ref.shape[1]
    half, group = cap // 2, total // 3
    acc = in_ref[0].astype(F32)
    for n in range(1, in_ref.shape[0]):
        acc = acc + in_ref[n].astype(F32)
    place = iota((total, 1), 0)
    block, line = place // (3 * half), place % (3 * half)
    source = line // half * group + block * half + line % half
    order = (source == iota((total, total), 1)).astype(F32).astype(BF16)
    out_ref[...] = jnp.dot(order, acc.astype(BF16), preferred_element_type=F32).astype(BF16)


def combine_kernel(in_ref, weights_ref, out_ref):
    odd = lax.rem(lax.axis_index("x"), 2) == 1
    count = out_ref.shape[0]
    sums = jnp.dot(weights_ref[...], in_ref[...], preferred_element_type=F32)
    sums = sums[: 3 * count] + sums[3 * count :]
    head = sums[:count]
    tail = sums[count : 2 * count, :HALF] + sums[2 * count :, HALF:]
    out = jnp.where(
        odd, jnp.concatenate([tail, head], axis=1), jnp.concatenate([head, tail], axis=1)
    )
    out_ref[...] = out.astype(BF16)


def call(kernel, shapes, *args, hbm=(), scratch=(), limit=16, flops=0, keep=False):
    vmem = pl.BlockSpec(memory_space=pltpu.VMEM)
    size = sum(a.size * a.dtype.itemsize for a in (*args, *hbm))
    outs = pl.pallas_call(
        kernel,
        out_shape=[(pltpu.VMEM if keep else jax.ShapeDtypeStruct)(shape, BF16) for shape in shapes],
        in_specs=[vmem] * len(args) + [pl.BlockSpec(memory_space=pltpu.HBM)] * len(hbm),
        out_specs=[vmem] * len(shapes),
        scratch_shapes=list(scratch),
        compiler_params=pltpu.CompilerParams(vmem_limit_bytes=limit * 1024 * 1024),
        cost_estimate=pl.CostEstimate(flops=flops, bytes_accessed=size, transcendentals=0),
    )(*args, *hbm)
    return outs if len(shapes) > 1 else outs[0]


def exchange_z(lines, slots):
    blocks = lines.reshape(slots, -1, 2, LANES)
    return lax.all_to_all(blocks, "z", split_axis=0, concat_axis=0, tiled=True).reshape(lines.shape)


def per_device(tokens, routes, gates, w_gate, w_up, w_down):
    slots, side = lax.axis_size("z"), lax.axis_size("x")
    shares = lax.axis_size("y") * side
    count, top = routes.shape
    cap = min(count, 2 * count * top // slots)
    total = slots * cap * 3 // 2
    rows = slots * cap
    plane = ("core", "y", "x")
    along = range(side)
    along_x = [[[c * shares + y * side + x for x in along] for y in along] for c in range(2)]
    along_y = [[[c * shares + y * side + x for y in along] for x in along] for c in range(2)]
    short = along_x[0] + along_y[1]
    long = along_y[0] + along_x[1]
    outgoing, weights, own = call(
        functools.partial(dispatch_kernel, slots, cap),
        [(total, LANES), (6 * count, total), (3, *w_down.shape[1:])],
        tokens,
        routes.T,
        gates.T,
        hbm=(w_gate.swapaxes(1, 2), w_up.swapaxes(1, 2), w_down),
        scratch=[pltpu.SemaphoreType.DMA((3,))],
        limit=54,
        keep=True,
    )
    other = lax.ppermute(own, "core", [(0, 1), (1, 0)])
    incoming = exchange_z(outgoing, slots)
    line = lax.all_gather(incoming, plane, axis_index_groups=short)
    copies = call(
        functools.partial(spread_kernel, cap), [(side, side, total, LANES)], line, limit=24
    )
    features = lax.all_to_all(
        copies, plane, split_axis=0, concat_axis=0, axis_index_groups=long, tiled=True
    )
    partials = call(
        ffn_kernel,
        [(shares, total, LANES)],
        features,
        own,
        other,
        scratch=[pltpu.VMEM((rows, shares * SHARE), BF16)],
        limit=32,
        flops=2 * rows * shares * SHARE * 6 * SHARE,
    )
    landed = lax.all_to_all(partials, ("y", "x"), split_axis=0, concat_axis=0, tiled=True)
    summed = call(functools.partial(sum_kernel, cap), [(total, LANES)], landed)
    returned = exchange_z(summed, slots)
    return call(combine_kernel, [(count, SHARE)], returned, weights)


def split_mesh(mesh):
    reps, shares = mesh.devices.shape
    side = int(round(shares**0.5))
    return Mesh(mesh.devices.reshape(reps // 2, 2, side, -1), ("z", "core", "y", "x"))


def solution(mesh):
    rep, tp = ("z", "core"), ("y", "x")
    in_specs = (
        P(rep, tp),
        P(rep, None),
        P(rep, None),
        P(rep, None, tp),
        P(rep, None, tp),
        P(rep, tp, None),
    )
    return jax.shard_map(
        per_device,
        mesh=split_mesh(mesh),
        in_specs=in_specs,
        out_specs=P(rep, tp),
        check_vma=False,
    )
```

```python
import functools

import jax
import jax.numpy as jnp
from jax import lax
from jax.experimental import pallas as pl
from jax.experimental.pallas import tpu as pltpu
from jax.sharding import Mesh
from jax.sharding import PartitionSpec as P

LANES = 128
HALF = LANES // 2
SHARE = LANES + HALF
F32 = jnp.float32
BF16 = jnp.bfloat16


def iota(shape, dim):
    return lax.broadcasted_iota(jnp.int32, shape, dim)


def lines_of(slot, place, cap):
    half, lines = cap // 2, 3 * cap // 2
    start = slot * lines
    head = start + place
    low = jnp.where(place < half, start + cap + place, -1)
    high = jnp.where(place < half, -1, start + cap + place - half)
    return head, low, high


def dispatch_kernel(
    slots,
    cap,
    tokens_ref,
    routes_ref,
    gates_ref,
    w_gate_ref,
    w_up_ref,
    w_down_ref,
    out_ref,
    weights_ref,
    own_ref,
    sems,
):
    copies = [
        pltpu.make_async_copy(ref.at[0], own_ref.at[n], sems.at[n])
        for n, ref in enumerate((w_gate_ref, w_up_ref, w_down_ref))
    ]
    for copy in copies:
        copy.start()
    odd = lax.rem(lax.axis_index("x"), 2) == 1
    count = tokens_ref.shape[0]
    top = routes_ref.shape[0]
    total = slots * cap * 3 // 2
    tok = tokens_ref[...].astype(F32)
    head = jnp.where(odd, tok[:, HALF:], tok[:, :LANES])
    tail = jnp.where(odd, tok[:, :HALF], tok[:, LANES:])
    both = jnp.concatenate([tail, tail], axis=1)
    left = iota((count, LANES), 1) < HALF
    chosen = [routes_ref[k : k + 1, :] for k in range(top)]
    slot_ids = iota((slots, count), 0)
    onehots = [chosen[k] == slot_ids for k in range(top)]
    named = functools.reduce(jnp.logical_or, onehots).astype(F32).astype(BF16)
    earlier = (iota((count, count), 0) < iota((count, count), 1)).astype(F32).astype(BF16)
    before = jnp.dot(named, earlier, preferred_element_type=F32)
    line_ids = iota((total, count), 0)
    lane_ids = iota((count, total), 1)
    diagonal = iota((count, count), 0) == iota((count, count), 1)

    def column(row):
        return jnp.sum(jnp.where(diagonal, row, 0.0), axis=1, keepdims=True)

    masks = [None, None, None]
    weights = [jnp.zeros((count, total), F32) for _ in range(3)]
    for k in range(top):
        place = jnp.sum(jnp.where(onehots[k], before, 0.0), axis=0, keepdims=True)
        slot_column = column(chosen[k].astype(F32)).astype(jnp.int32)
        place_column = column(place).astype(jnp.int32)
        gate_column = column(gates_ref[k : k + 1, :])
        place = place.astype(jnp.int32)
        for n, line in enumerate(lines_of(chosen[k], place, cap)):
            hit = line_ids == line
            masks[n] = hit if masks[n] is None else jnp.logical_or(masks[n], hit)
        for n, line in enumerate(lines_of(slot_column, place_column, cap)):
            weights[n] = jnp.where(lane_ids == line, gate_column, weights[n])
    parts = (head, jnp.where(left, both, 0.0), jnp.where(left, 0.0, both))
    out = jnp.zeros((total, LANES), F32)
    for mask, part in zip(masks, parts):
        out = out + jnp.dot(
            mask.astype(F32).astype(BF16), part.astype(BF16), preferred_element_type=F32
        )
    out_ref[...] = out.astype(BF16)
    for n, weight in enumerate(weights):
        coarse = weight.astype(BF16)
        weights_ref[n * count : (n + 1) * count, :] = coarse
        weights_ref[(n + 3) * count : (n + 4) * count, :] = (weight - coarse.astype(F32)).astype(
            BF16
        )
    for copy in copies:
        copy.wait()


def spread_kernel(cap, in_ref, out_ref):
    total = in_ref.shape[1]
    half, group = cap // 2, total // 3
    place = iota((total, 1), 0)
    kind, rest = place // group, place % group
    source = rest // half * (3 * half) + rest % half + kind * half
    order = (source == iota((total, total), 1)).astype(F32).astype(BF16)
    for share in range(in_ref.shape[0]):
        lines = jnp.dot(order, in_ref[share], preferred_element_type=F32).astype(BF16)
        for n in range(out_ref.shape[0]):
            out_ref[n, share] = lines


def ffn_kernel(x_ref, own_ref, other_hbm, out_ref, rows_ref, other_ref, sem):
    copy = pltpu.make_async_copy(other_hbm, other_ref, sem)
    copy.start()
    rows = rows_ref.shape[0]
    mid = rows // 2
    left = iota((mid, LANES), 1) < HALF
    pairs = out_ref.shape[0] // 2
    wide = 3 * LANES
    for n in range(pairs):
        start = n * wide
        rows_ref[:, start : start + LANES] = x_ref[2 * n, :rows, :]
        rows_ref[:, start + 2 * LANES : start + wide] = x_ref[2 * n + 1, :rows, :]
        a = x_ref[2 * n, rows:, :].astype(F32)
        b = x_ref[2 * n + 1, rows:, :].astype(F32)
        upper = jnp.where(left, a, pltpu.roll(b, HALF, 1))
        lower = jnp.where(left, pltpu.roll(a, HALF, 1), b)
        rows_ref[:mid, start + LANES : start + 2 * LANES] = upper.astype(BF16)
        rows_ref[mid:, start + LANES : start + 2 * LANES] = lower.astype(BF16)
    hidden = []
    last = (((1,), (1,)), ((), ()))
    for ref in (own_ref, other_ref):
        if ref is other_ref:
            copy.wait()
        gate = lax.dot_general(rows_ref[...], ref[0], last, preferred_element_type=F32)
        up = lax.dot_general(rows_ref[...], ref[1], last, preferred_element_type=F32)
        hidden.append((gate / (1.0 + jnp.exp(-gate)) * up).astype(BF16))
    for n in range(pairs):
        start = n * wide
        out = jnp.dot(hidden[0], own_ref[2, :, start : start + wide], preferred_element_type=F32)
        out = out + jnp.dot(
            hidden[1], other_ref[2, :, start : start + wide], preferred_element_type=F32
        )
        out_ref[2 * n, :rows, :] = out[:, :LANES].astype(BF16)
        out_ref[2 * n + 1, :rows, :] = out[:, 2 * LANES :].astype(BF16)
        upper, lower = out[:mid, LANES : 2 * LANES], out[mid:, LANES : 2 * LANES]
        out_ref[2 * n, rows:, :] = jnp.where(left, upper, pltpu.roll(lower, HALF, 1)).astype(BF16)
        out_ref[2 * n + 1, rows:, :] = jnp.where(left, pltpu.roll(upper, HALF, 1), lower).astype(
            BF16
        )


def sum_kernel(cap, in_ref, out_ref):
    total = in_ref.shape[1]
    half, group = cap // 2, total // 3
    acc = in_ref[0].astype(F32)
    for n in range(1, in_ref.shape[0]):
        acc = acc + in_ref[n].astype(F32)
    place = iota((total, 1), 0)
    block, line = place // (3 * half), place % (3 * half)
    source = line // half * group + block * half + line % half
    order = (source == iota((total, total), 1)).astype(F32).astype(BF16)
    out_ref[...] = jnp.dot(order, acc.astype(BF16), preferred_element_type=F32).astype(BF16)


def combine_kernel(in_ref, weights_ref, out_ref):
    odd = lax.rem(lax.axis_index("x"), 2) == 1
    count = out_ref.shape[0]
    sums = jnp.dot(weights_ref[...], in_ref[...], preferred_element_type=F32)
    sums = sums[: 3 * count] + sums[3 * count :]
    head = sums[:count]
    tail = sums[count : 2 * count, :HALF] + sums[2 * count :, HALF:]
    out = jnp.where(
        odd, jnp.concatenate([tail, head], axis=1), jnp.concatenate([head, tail], axis=1)
    )
    out_ref[...] = out.astype(BF16)


def call(kernel, shapes, *args, hbm=(), scratch=(), limit=16, flops=0, keep=None):
    vmem = pl.BlockSpec(memory_space=pltpu.VMEM)
    size = sum(a.size * a.dtype.itemsize for a in (*args, *hbm))
    outs = pl.pallas_call(
        kernel,
        out_shape=[
            (pltpu.VMEM if n == keep else jax.ShapeDtypeStruct)(shape, BF16)
            for n, shape in enumerate(shapes)
        ],
        in_specs=[vmem] * len(args) + [pl.BlockSpec(memory_space=pltpu.HBM)] * len(hbm),
        out_specs=[vmem] * len(shapes),
        scratch_shapes=list(scratch),
        compiler_params=pltpu.CompilerParams(vmem_limit_bytes=limit * 1024 * 1024),
        cost_estimate=pl.CostEstimate(flops=flops, bytes_accessed=size, transcendentals=0),
    )(*args, *hbm)
    return outs if len(shapes) > 1 else outs[0]


def exchange_z(lines, slots):
    blocks = lines.reshape(slots, -1, 2, LANES)
    return lax.all_to_all(blocks, "z", split_axis=0, concat_axis=0, tiled=True).reshape(lines.shape)


def spread(cap, lines, copies):
    shape = (copies, *lines.shape)
    return call(functools.partial(spread_kernel, cap), [shape], lines, limit=24)


def gather_in_steps(cap, lines):
    side = lax.axis_size("x")
    copies = spread(cap, lax.all_gather(lines, "x"), side)
    features = lax.all_to_all(copies, "y", split_axis=0, concat_axis=0, tiled=True)
    return features.reshape(-1, *lines.shape)


def gather_at_once(cap, lines):
    copies = spread(cap, lines[None], lax.axis_size("y") * lax.axis_size("x"))
    features = lax.all_to_all(copies, ("y", "x"), split_axis=0, concat_axis=0, tiled=True)
    return features.reshape(-1, *lines.shape)


def per_device(tokens, routes, gates, w_gate, w_up, w_down):
    slots = lax.axis_size("z")
    shares = lax.axis_size("y") * lax.axis_size("x")
    count, top = routes.shape
    cap = min(count, 2 * count * top // slots)
    total = slots * cap * 3 // 2
    rows = slots * cap
    outgoing, weights, own = call(
        functools.partial(dispatch_kernel, slots, cap),
        [(total, LANES), (6 * count, total), (3, *w_down.shape[1:])],
        tokens,
        routes.T,
        gates.T,
        hbm=(w_gate.swapaxes(1, 2), w_up.swapaxes(1, 2), w_down),
        scratch=[pltpu.SemaphoreType.DMA((3,))],
        limit=54,
        keep=2,
    )
    other = lax.ppermute(own, "core", [(0, 1), (1, 0)])
    outgoing, core = lax.optimization_barrier((outgoing, lax.axis_index("core")))
    incoming, core = lax.optimization_barrier((exchange_z(outgoing, slots), core))
    def finish(gather):
        features = gather(cap, incoming)
        partials = call(
            ffn_kernel,
            [(shares, total, LANES)],
            features,
            own,
            hbm=(other,),
            scratch=[
                pltpu.VMEM((rows, shares * SHARE), BF16),
                pltpu.VMEM(other.shape, BF16),
                pltpu.SemaphoreType.DMA,
            ],
            limit=40,
            flops=2 * rows * shares * SHARE * 6 * SHARE,
        )
        landed = lax.all_to_all(partials, ("y", "x"), split_axis=0, concat_axis=0, tiled=True)
        summed = call(functools.partial(sum_kernel, cap), [(total, LANES)], landed)
        returned = exchange_z(summed, slots)
        return call(combine_kernel, [(count, SHARE)], returned, weights)

    return lax.cond(
        core == 0,
        functools.partial(finish, gather_in_steps),
        functools.partial(finish, gather_at_once),
    )


def split_mesh(mesh):
    reps, shares = mesh.devices.shape
    side = int(round(shares**0.5))
    return Mesh(mesh.devices.reshape(reps // 2, 2, side, -1), ("z", "core", "y", "x"))


def solution(mesh):
    rep, tp = ("z", "core"), ("y", "x")
    in_specs = (
        P(rep, tp),
        P(rep, None),
        P(rep, None),
        P(rep, None, tp),
        P(rep, None, tp),
        P(rep, tp, None),
    )
    return jax.shard_map(
        per_device,
        mesh=split_mesh(mesh),
        in_specs=in_specs,
        out_specs=P(rep, tp),
        check_vma=False,
    )
```

```python
import functools

import jax
import jax.numpy as jnp
from jax import lax
from jax.experimental import pallas as pl
from jax.experimental.pallas import tpu as pltpu
from jax.sharding import Mesh
from jax.sharding import PartitionSpec as P

LANES = 128
HALF = LANES // 2
SHARE = LANES + HALF
F32 = jnp.float32
BF16 = jnp.bfloat16


def iota(shape, dim):
    return lax.broadcasted_iota(jnp.int32, shape, dim)


def lines_of(slot, place, cap):
    half, lines = cap // 2, 3 * cap // 2
    start = slot * lines
    head = start + place
    low = jnp.where(place < half, start + cap + place, -1)
    high = jnp.where(place < half, -1, start + cap + place - half)
    return head, low, high


def line_orders(total, cap):
    half, group = cap // 2, total // 3
    place, line_ids = iota((total, 1), 0), iota((total, total), 1)
    kind, rest = place // group, place % group
    source = rest // half * (3 * half) + rest % half + kind * half
    block, line = place // (3 * half), place % (3 * half)
    target = line // half * group + block * half + line % half
    return [(index == line_ids).astype(F32).astype(BF16) for index in (source, target)]


def dispatch_kernel(
    slots,
    cap,
    tokens_hbm,
    routes_hbm,
    gates_hbm,
    w_gate_ref,
    w_up_ref,
    w_down_ref,
    out_ref,
    weights_ref,
    own_ref,
    order_ref,
    back_ref,
    tokens_ref,
    routes_ref,
    gates_ref,
    small_sems,
    sems,
):
    small = [
        pltpu.make_async_copy(source, target, small_sems.at[n])
        for n, (source, target) in enumerate(
            ((tokens_hbm, tokens_ref), (routes_hbm, routes_ref), (gates_hbm, gates_ref))
        )
    ]
    copies = [
        pltpu.make_async_copy(ref.at[0], own_ref.at[n], sems.at[n])
        for n, ref in enumerate((w_gate_ref, w_up_ref, w_down_ref))
    ]
    for copy in small + copies:
        copy.start()
    order_ref[...], back_ref[...] = line_orders(order_ref.shape[0], cap)
    for copy in small:
        copy.wait()
    odd = lax.rem(lax.axis_index("x"), 2) == 1
    count = tokens_ref.shape[0]
    top = routes_ref.shape[0]
    total = slots * cap * 3 // 2
    tok = tokens_ref[...].astype(F32)
    head = jnp.where(odd, tok[:, HALF:], tok[:, :LANES])
    tail = jnp.where(odd, tok[:, :HALF], tok[:, LANES:])
    both = jnp.concatenate([tail, tail], axis=1)
    left = iota((count, LANES), 1) < HALF
    chosen = [routes_ref[k : k + 1, :] for k in range(top)]
    slot_ids = iota((slots, count), 0)
    onehots = [chosen[k] == slot_ids for k in range(top)]
    named = functools.reduce(jnp.logical_or, onehots).astype(F32).astype(BF16)
    earlier = (iota((count, count), 0) < iota((count, count), 1)).astype(F32).astype(BF16)
    before = jnp.dot(named, earlier, preferred_element_type=F32)
    line_ids = iota((total, count), 0)
    lane_ids = iota((count, total), 1)
    diagonal = iota((count, count), 0) == iota((count, count), 1)

    def column(row):
        return jnp.sum(jnp.where(diagonal, row, 0.0), axis=1, keepdims=True)

    masks = [None, None, None]
    weights = [jnp.zeros((count, total), F32) for _ in range(3)]
    for k in range(top):
        place = jnp.sum(jnp.where(onehots[k], before, 0.0), axis=0, keepdims=True)
        slot_column = column(chosen[k].astype(F32)).astype(jnp.int32)
        place_column = column(place).astype(jnp.int32)
        gate_column = column(gates_ref[k : k + 1, :])
        place = place.astype(jnp.int32)
        for n, line in enumerate(lines_of(chosen[k], place, cap)):
            hit = line_ids == line
            masks[n] = hit if masks[n] is None else jnp.logical_or(masks[n], hit)
        for n, line in enumerate(lines_of(slot_column, place_column, cap)):
            weights[n] = jnp.where(lane_ids == line, gate_column, weights[n])
    parts = (head, jnp.where(left, both, 0.0), jnp.where(left, 0.0, both))
    out = jnp.zeros((total, LANES), F32)
    for mask, part in zip(masks, parts):
        out = out + jnp.dot(
            mask.astype(F32).astype(BF16), part.astype(BF16), preferred_element_type=F32
        )
    out_ref[...] = out.astype(BF16)
    for n, weight in enumerate(weights):
        coarse = weight.astype(BF16)
        weights_ref[n * count : (n + 1) * count, :] = coarse
        weights_ref[(n + 3) * count : (n + 4) * count, :] = (weight - coarse.astype(F32)).astype(
            BF16
        )
    for copy in copies:
        copy.wait()


def spread_kernel(in_ref, order_ref, out_ref):
    for share in range(in_ref.shape[0]):
        lines = jnp.dot(order_ref[...], in_ref[share], preferred_element_type=F32).astype(BF16)
        for n in range(out_ref.shape[0]):
            out_ref[n, share] = lines


def ffn_kernel(x_ref, own_ref, other_ref, out_ref, rows_ref):
    side = x_ref.shape[0]
    first = lax.axis_index("core") == 1

    def block(n):
        y, x = n // side, n % side
        return jnp.where(first, y, x), jnp.where(first, x, y)

    rows = rows_ref.shape[0]
    mid = rows // 2
    left = iota((mid, LANES), 1) < HALF
    pairs = out_ref.shape[0] // 2
    wide = 3 * LANES
    for n in range(pairs):
        start = n * wide
        even, odd = block(2 * n), block(2 * n + 1)
        rows_ref[:, start : start + LANES] = x_ref[even[0], even[1], :rows, :]
        rows_ref[:, start + 2 * LANES : start + wide] = x_ref[odd[0], odd[1], :rows, :]
        a = x_ref[even[0], even[1], rows:, :].astype(F32)
        b = x_ref[odd[0], odd[1], rows:, :].astype(F32)
        upper = jnp.where(left, a, pltpu.roll(b, HALF, 1))
        lower = jnp.where(left, pltpu.roll(a, HALF, 1), b)
        rows_ref[:mid, start + LANES : start + 2 * LANES] = upper.astype(BF16)
        rows_ref[mid:, start + LANES : start + 2 * LANES] = lower.astype(BF16)
    hidden = []
    last = (((1,), (1,)), ((), ()))
    for gates, ups in ((own_ref[0], own_ref[1]), (other_ref[0], other_ref[1])):
        gate = lax.dot_general(rows_ref[...], gates, last, preferred_element_type=F32)
        up = lax.dot_general(rows_ref[...], ups, last, preferred_element_type=F32)
        hidden.append((gate / (1.0 + jnp.exp(-gate)) * up).astype(BF16))
    for n in range(pairs):
        start = n * wide
        out = jnp.dot(hidden[0], own_ref[2, :, start : start + wide], preferred_element_type=F32)
        out = out + jnp.dot(
            hidden[1], other_ref[2, :, start : start + wide], preferred_element_type=F32
        )
        out_ref[2 * n, :rows, :] = out[:, :LANES].astype(BF16)
        out_ref[2 * n + 1, :rows, :] = out[:, 2 * LANES :].astype(BF16)
        upper, lower = out[:mid, LANES : 2 * LANES], out[mid:, LANES : 2 * LANES]
        out_ref[2 * n, rows:, :] = jnp.where(left, upper, pltpu.roll(lower, HALF, 1)).astype(BF16)
        out_ref[2 * n + 1, rows:, :] = jnp.where(left, pltpu.roll(upper, HALF, 1), lower).astype(
            BF16
        )


def sum_kernel(in_ref, order_ref, out_ref):
    acc = in_ref[0].astype(F32)
    for n in range(1, in_ref.shape[0]):
        acc = acc + in_ref[n].astype(F32)
    out = jnp.dot(order_ref[...], acc.astype(BF16), preferred_element_type=F32)
    out_ref[...] = out.astype(BF16)


def combine_kernel(in_ref, weights_ref, out_ref):
    odd = lax.rem(lax.axis_index("x"), 2) == 1
    count = out_ref.shape[0]
    sums = jnp.dot(weights_ref[...], in_ref[...], preferred_element_type=F32)
    sums = sums[: 3 * count] + sums[3 * count :]
    head = sums[:count]
    tail = sums[count : 2 * count, :HALF] + sums[2 * count :, HALF:]
    out = jnp.where(
        odd, jnp.concatenate([tail, head], axis=1), jnp.concatenate([head, tail], axis=1)
    )
    out_ref[...] = out.astype(BF16)


def call(kernel, shapes, *args, hbm=(), scratch=(), limit=16, flops=0, keep=()):
    vmem = pl.BlockSpec(memory_space=pltpu.VMEM)
    size = sum(a.size * a.dtype.itemsize for a in (*args, *hbm))
    outs = pl.pallas_call(
        kernel,
        out_shape=[
            (pltpu.VMEM if n in keep else jax.ShapeDtypeStruct)(shape, BF16)
            for n, shape in enumerate(shapes)
        ],
        in_specs=[vmem] * len(args) + [pl.BlockSpec(memory_space=pltpu.HBM)] * len(hbm),
        out_specs=[vmem] * len(shapes),
        scratch_shapes=list(scratch),
        compiler_params=pltpu.CompilerParams(vmem_limit_bytes=limit * 1024 * 1024),
        cost_estimate=pl.CostEstimate(flops=flops, bytes_accessed=size, transcendentals=0),
    )(*args, *hbm)
    return outs if len(shapes) > 1 else outs[0]


def exchange_z(lines, slots):
    blocks = lines.reshape(slots, -1, 2, LANES)
    return lax.all_to_all(blocks, "z", split_axis=0, concat_axis=0, tiled=True).reshape(lines.shape)


def per_device(tokens, routes, gates, w_gate, w_up, w_down):
    slots, side = lax.axis_size("z"), lax.axis_size("x")
    shares = lax.axis_size("y") * side
    count, top = routes.shape
    cap = min(count, 2 * count * top // slots)
    total = slots * cap * 3 // 2
    rows = slots * cap
    plane = ("core", "y", "x")
    along = range(side)
    along_x = [[[c * shares + y * side + x for x in along] for y in along] for c in range(2)]
    along_y = [[[c * shares + y * side + x for y in along] for x in along] for c in range(2)]
    short = along_y[0] + along_x[1]
    long = along_x[0] + along_y[1]
    outgoing, weights, own, order, back = call(
        functools.partial(dispatch_kernel, slots, cap),
        [
            (total, LANES),
            (6 * count, total),
            (3, *w_down.shape[1:]),
            (total, total),
            (total, total),
        ],
        hbm=(
            tokens,
            routes.T,
            gates.T,
            w_gate.swapaxes(1, 2),
            w_up.swapaxes(1, 2),
            w_down,
        ),
        scratch=[
            pltpu.VMEM(tokens.shape, BF16),
            pltpu.VMEM((top, count), jnp.int32),
            pltpu.VMEM((top, count), F32),
            pltpu.SemaphoreType.DMA((3,)),
            pltpu.SemaphoreType.DMA((3,)),
        ],
        limit=54,
        keep=range(5),
    )
    other = lax.ppermute(own, "core", [(0, 1), (1, 0)])
    incoming = exchange_z(outgoing, slots)
    line = lax.all_gather(incoming, plane, axis_index_groups=short)
    copies = call(spread_kernel, [(side, side, total, LANES)], line, order, limit=24)
    features = lax.all_to_all(
        copies, plane, split_axis=0, concat_axis=0, axis_index_groups=long, tiled=True
    )
    partials = call(
        ffn_kernel,
        [(shares, total, LANES)],
        features,
        own,
        other,
        scratch=[pltpu.VMEM((rows, shares * SHARE), BF16)],
        limit=32,
        flops=2 * rows * shares * SHARE * 6 * SHARE,
    )
    landed = lax.all_to_all(partials, ("y", "x"), split_axis=0, concat_axis=0, tiled=True)
    summed = call(sum_kernel, [(total, LANES)], landed, back)
    returned = exchange_z(summed, slots)
    return call(combine_kernel, [(count, SHARE)], returned, weights)


def split_mesh(mesh):
    reps, shares = mesh.devices.shape
    side = int(round(shares**0.5))
    return Mesh(mesh.devices.reshape(reps // 2, 2, side, -1), ("z", "core", "y", "x"))


def solution(mesh):
    rep, tp = ("z", "core"), ("y", "x")
    in_specs = (
        P(rep, tp),
        P(rep, None),
        P(rep, None),
        P(rep, None, tp),
        P(rep, None, tp),
        P(rep, tp, None),
    )
    return jax.shard_map(
        per_device,
        mesh=split_mesh(mesh),
        in_specs=in_specs,
        out_specs=P(rep, tp),
        check_vma=False,
    )
```

```python
import functools

import jax
import jax.numpy as jnp
from jax import lax
from jax.experimental import pallas as pl
from jax.experimental.pallas import tpu as pltpu
from jax.sharding import Mesh
from jax.sharding import PartitionSpec as P

LANES = 128
HALF = LANES // 2
SHARE = LANES + HALF
F32 = jnp.float32
BF16 = jnp.bfloat16


def iota(shape, dim):
    return lax.broadcasted_iota(jnp.int32, shape, dim)


def lines_of(slot, place, cap):
    half, lines = cap // 2, 3 * cap // 2
    start = slot * lines
    head = start + place
    low = jnp.where(place < half, start + cap + place, -1)
    high = jnp.where(place < half, -1, start + cap + place - half)
    return head, low, high


def line_orders(total, cap):
    half, group = cap // 2, total // 3
    place, line_ids = iota((total, 1), 0), iota((total, total), 1)
    kind, rest = place // group, place % group
    source = rest // half * (3 * half) + rest % half + kind * half
    block, line = place // (3 * half), place % (3 * half)
    target = line // half * group + block * half + line % half
    return [(index == line_ids).astype(F32).astype(BF16) for index in (source, target)]


def dispatch_kernel(
    slots,
    cap,
    tokens_hbm,
    routes_hbm,
    gates_hbm,
    w_gate_ref,
    w_up_ref,
    w_down_ref,
    out_ref,
    weights_ref,
    own_ref,
    order_ref,
    back_ref,
    tokens_ref,
    routes_ref,
    gates_ref,
    small_sems,
    sems,
):
    small = [
        pltpu.make_async_copy(source, target, small_sems.at[n])
        for n, (source, target) in enumerate(
            ((tokens_hbm, tokens_ref), (routes_hbm, routes_ref), (gates_hbm, gates_ref))
        )
    ]
    copies = [
        pltpu.make_async_copy(ref.at[0], own_ref.at[n], sems.at[n])
        for n, ref in enumerate((w_gate_ref, w_up_ref, w_down_ref))
    ]
    for copy in small + copies:
        copy.start()
    order_ref[...], back_ref[...] = line_orders(order_ref.shape[0], cap)
    for copy in small:
        copy.wait()
    odd = lax.rem(lax.axis_index("x"), 2) == 1
    count = tokens_ref.shape[0]
    top = routes_ref.shape[0]
    total = slots * cap * 3 // 2
    tok = tokens_ref[...].astype(F32)
    head = jnp.where(odd, tok[:, HALF:], tok[:, :LANES])
    tail = jnp.where(odd, tok[:, :HALF], tok[:, LANES:])
    both = jnp.concatenate([tail, tail], axis=1)
    left = iota((count, LANES), 1) < HALF
    chosen = [routes_ref[k : k + 1, :] for k in range(top)]
    slot_ids = iota((slots, count), 0)
    onehots = [chosen[k] == slot_ids for k in range(top)]
    named = functools.reduce(jnp.logical_or, onehots).astype(F32).astype(BF16)
    earlier = (iota((count, count), 0) < iota((count, count), 1)).astype(F32).astype(BF16)
    before = jnp.dot(named, earlier, preferred_element_type=F32)
    line_ids = iota((total, count), 0)
    lane_ids = iota((count, total), 1)
    diagonal = iota((count, count), 0) == iota((count, count), 1)

    def column(row):
        return jnp.sum(jnp.where(diagonal, row, 0.0), axis=1, keepdims=True)

    masks = [None, None, None]
    weights = [jnp.zeros((count, total), F32) for _ in range(3)]
    for k in range(top):
        place = jnp.sum(jnp.where(onehots[k], before, 0.0), axis=0, keepdims=True)
        slot_column = column(chosen[k].astype(F32)).astype(jnp.int32)
        place_column = column(place).astype(jnp.int32)
        gate_column = column(gates_ref[k : k + 1, :])
        place = place.astype(jnp.int32)
        for n, line in enumerate(lines_of(chosen[k], place, cap)):
            hit = line_ids == line
            masks[n] = hit if masks[n] is None else jnp.logical_or(masks[n], hit)
        for n, line in enumerate(lines_of(slot_column, place_column, cap)):
            weights[n] = jnp.where(lane_ids == line, gate_column, weights[n])
    parts = (head, jnp.where(left, both, 0.0), jnp.where(left, 0.0, both))
    out = jnp.zeros((total, LANES), F32)
    for mask, part in zip(masks, parts):
        out = out + jnp.dot(
            mask.astype(F32).astype(BF16), part.astype(BF16), preferred_element_type=F32
        )
    out_ref[...] = out.astype(BF16)
    for n, weight in enumerate(weights):
        coarse = weight.astype(BF16)
        weights_ref[n * count : (n + 1) * count, :] = coarse
        weights_ref[(n + 3) * count : (n + 4) * count, :] = (weight - coarse.astype(F32)).astype(
            BF16
        )
    for copy in copies:
        copy.wait()


def spread_kernel(in_ref, order_ref, out_ref):
    for share in range(in_ref.shape[0]):
        lines = jnp.dot(order_ref[...], in_ref[share], preferred_element_type=F32).astype(BF16)
        for n in range(out_ref.shape[0]):
            out_ref[n, share] = lines


def ffn_kernel(x_ref, own_ref, other_ref, out_ref, rows_ref):
    side = x_ref.shape[0]
    first = lax.axis_index("core") == 0

    def block(n):
        y, x = n // side, n % side
        return jnp.where(first, y, x), jnp.where(first, x, y)

    rows = rows_ref.shape[0]
    mid = rows // 2
    left = iota((mid, LANES), 1) < HALF
    pairs = out_ref.shape[0] // 2
    wide = 3 * LANES
    for n in range(pairs):
        start = n * wide
        even, odd = block(2 * n), block(2 * n + 1)
        rows_ref[:, start : start + LANES] = x_ref[even[0], even[1], :rows, :]
        rows_ref[:, start + 2 * LANES : start + wide] = x_ref[odd[0], odd[1], :rows, :]
        a = x_ref[even[0], even[1], rows:, :].astype(F32)
        b = x_ref[odd[0], odd[1], rows:, :].astype(F32)
        upper = jnp.where(left, a, pltpu.roll(b, HALF, 1))
        lower = jnp.where(left, pltpu.roll(a, HALF, 1), b)
        rows_ref[:mid, start + LANES : start + 2 * LANES] = upper.astype(BF16)
        rows_ref[mid:, start + LANES : start + 2 * LANES] = lower.astype(BF16)
    hidden = []
    last = (((1,), (1,)), ((), ()))
    for gates, ups in ((own_ref[0], own_ref[1]), (other_ref[0], other_ref[1])):
        gate = lax.dot_general(rows_ref[...], gates, last, preferred_element_type=F32)
        up = lax.dot_general(rows_ref[...], ups, last, preferred_element_type=F32)
        hidden.append((gate / (1.0 + jnp.exp(-gate)) * up).astype(BF16))
    for n in range(pairs):
        start = n * wide
        out = jnp.dot(hidden[0], own_ref[2, :, start : start + wide], preferred_element_type=F32)
        out = out + jnp.dot(
            hidden[1], other_ref[2, :, start : start + wide], preferred_element_type=F32
        )
        out_ref[2 * n, :rows, :] = out[:, :LANES].astype(BF16)
        out_ref[2 * n + 1, :rows, :] = out[:, 2 * LANES :].astype(BF16)
        upper, lower = out[:mid, LANES : 2 * LANES], out[mid:, LANES : 2 * LANES]
        out_ref[2 * n, rows:, :] = jnp.where(left, upper, pltpu.roll(lower, HALF, 1)).astype(BF16)
        out_ref[2 * n + 1, rows:, :] = jnp.where(left, pltpu.roll(upper, HALF, 1), lower).astype(
            BF16
        )


def sum_kernel(in_ref, order_ref, out_ref):
    acc = in_ref[0].astype(F32)
    for n in range(1, in_ref.shape[0]):
        acc = acc + in_ref[n].astype(F32)
    out = jnp.dot(order_ref[...], acc.astype(BF16), preferred_element_type=F32)
    out_ref[...] = out.astype(BF16)


def combine_kernel(in_ref, weights_ref, out_ref):
    odd = lax.rem(lax.axis_index("x"), 2) == 1
    count = out_ref.shape[0]
    sums = jnp.dot(weights_ref[...], in_ref[...], preferred_element_type=F32)
    sums = sums[: 3 * count] + sums[3 * count :]
    head = sums[:count]
    tail = sums[count : 2 * count, :HALF] + sums[2 * count :, HALF:]
    out = jnp.where(
        odd, jnp.concatenate([tail, head], axis=1), jnp.concatenate([head, tail], axis=1)
    )
    out_ref[...] = out.astype(BF16)


def call(kernel, shapes, *args, hbm=(), scratch=(), limit=16, flops=0, keep=()):
    vmem = pl.BlockSpec(memory_space=pltpu.VMEM)
    size = sum(a.size * a.dtype.itemsize for a in (*args, *hbm))
    outs = pl.pallas_call(
        kernel,
        out_shape=[
            (pltpu.VMEM if n in keep else jax.ShapeDtypeStruct)(shape, BF16)
            for n, shape in enumerate(shapes)
        ],
        in_specs=[vmem] * len(args) + [pl.BlockSpec(memory_space=pltpu.HBM)] * len(hbm),
        out_specs=[vmem] * len(shapes),
        scratch_shapes=list(scratch),
        compiler_params=pltpu.CompilerParams(vmem_limit_bytes=limit * 1024 * 1024),
        cost_estimate=pl.CostEstimate(flops=flops, bytes_accessed=size, transcendentals=0),
    )(*args, *hbm)
    return outs if len(shapes) > 1 else outs[0]


def exchange_z(lines, slots):
    blocks = lines.reshape(slots, -1, 2, LANES)
    return lax.all_to_all(blocks, "z", split_axis=0, concat_axis=0, tiled=True).reshape(lines.shape)


def per_device(tokens, routes, gates, w_gate, w_up, w_down):
    slots, side = lax.axis_size("z"), lax.axis_size("x")
    shares = lax.axis_size("y") * side
    count, top = routes.shape
    cap = min(count, 2 * count * top // slots)
    total = slots * cap * 3 // 2
    rows = slots * cap
    plane = ("core", "y", "x")
    along = range(side)
    along_x = [[[c * shares + y * side + x for x in along] for y in along] for c in range(2)]
    along_y = [[[c * shares + y * side + x for y in along] for x in along] for c in range(2)]
    short = along_x[0] + along_y[1]
    long = along_y[0] + along_x[1]
    outgoing, weights, own, order, back = call(
        functools.partial(dispatch_kernel, slots, cap),
        [
            (total, LANES),
            (6 * count, total),
            (3, *w_down.shape[1:]),
            (total, total),
            (total, total),
        ],
        hbm=(
            tokens,
            routes.T,
            gates.T,
            w_gate.swapaxes(1, 2),
            w_up.swapaxes(1, 2),
            w_down,
        ),
        scratch=[
            pltpu.VMEM(tokens.shape, BF16),
            pltpu.VMEM((top, count), jnp.int32),
            pltpu.VMEM((top, count), F32),
            pltpu.SemaphoreType.DMA((3,)),
            pltpu.SemaphoreType.DMA((3,)),
        ],
        limit=54,
        keep=range(5),
    )
    other = lax.ppermute(own, "core", [(0, 1), (1, 0)])
    incoming = exchange_z(outgoing, slots)
    line = lax.all_gather(incoming, plane, axis_index_groups=short)
    copies = call(spread_kernel, [(side, side, total, LANES)], line, order, limit=24)
    features = lax.all_to_all(
        copies, plane, split_axis=0, concat_axis=0, axis_index_groups=long, tiled=True
    )
    partials = call(
        ffn_kernel,
        [(shares, total, LANES)],
        features,
        own,
        other,
        scratch=[pltpu.VMEM((rows, shares * SHARE), BF16)],
        limit=32,
        flops=2 * rows * shares * SHARE * 6 * SHARE,
    )
    landed = lax.all_to_all(partials, ("y", "x"), split_axis=0, concat_axis=0, tiled=True)
    summed = call(sum_kernel, [(total, LANES)], landed, back)
    returned = exchange_z(summed, slots)
    return call(combine_kernel, [(count, SHARE)], returned, weights)


def split_mesh(mesh):
    reps, shares = mesh.devices.shape
    side = int(round(shares**0.5))
    return Mesh(mesh.devices.reshape(reps // 2, 2, side, -1), ("z", "core", "y", "x"))


def solution(mesh):
    rep, tp = ("z", "core"), ("y", "x")
    in_specs = (
        P(rep, tp),
        P(rep, None),
        P(rep, None),
        P(rep, None, tp),
        P(rep, None, tp),
        P(rep, tp, None),
    )
    return jax.shard_map(
        per_device,
        mesh=split_mesh(mesh),
        in_specs=in_specs,
        out_specs=P(rep, tp),
        check_vma=False,
    )
```
